32 devices in a mesh: slab: 8 (over z, y), energy: 4 (over x, core).
Axes of the slice: x: 2, y: 2, z: 4, core: 2. Of those that a mesh axis runs over, the one named last changes fastest.
Arguments:
- source: float32 [16, 2, 8, 192, 128], P('slab', None, 'energy'), may hold values from -1.2 to 1.2
- onsite_block: float32 [192, 192], replicated, may hold values from -1.3 to 1.3, as said below
- hopping_block: float32 [192, 192], replicated, may hold values from -0.5 to 1.5
- potential_table: float32 [16, 192], replicated, may hold values from -0.5 to 0.5
- slab_profile: int32 [16], P('slab'), may hold values from 0 to 15
- occupation: float32 [16, 8, 192], P('slab', 'energy'), may hold values from 0.1 to 1
- coupling: float32 [4], replicated, may hold values from 0.02 to 0.08
- phonon_shift: int32 [4], replicated, may hold values from 1 to 2, as said below
Outputs:
- amplitude: float32 [16, 2, 8, 192, 128], P('slab', None, 'energy')
- density: float32 [16, 8, 192], P('slab', 'energy')
The draws below stay inside these ranges and needn't reach their ends.
Inputs may be any that keep to these rules, and one draw needn't show every extreme that they name: `phonon_shift`: some mode shifts by exactly 2 points and some by exactly 1. `onsite_block`: symmetric.
All inputs are finite; a program needn't handle non-finite values.
Results may differ from the reference program's by a relative error of at most 0.0003.
Values sent between devices are 32-bit elements; how exact they have to be, the bound alone decides.
A program may use at most 128 MiB of HBM per device.

```python
import math
import jax
import jax.numpy as jnp
from jax import lax

ORBITALS = 192
COLUMNS = 128
ENERGY_DEV = 2
LEVELS = 16
PHONON_MODES = 4
SLABS = 16
ENERGIES = 8


def draw_onsite_block(key, part):
    key = jax.random.fold_in(key, 101)
    key_diag, key_off = jax.random.split(key)
    spread = 0.3 / jnp.sqrt(ORBITALS * 1.0)
    diagonal = jax.random.uniform(key_diag, (ORBITALS,), jnp.float32, -0.8, 0.8)
    rough = jnp.clip(jax.random.normal(key_off, (ORBITALS, ORBITALS), jnp.float32), -4.0, 4.0)
    return 0.5 * spread * (rough + rough.T) + jnp.diag(diagonal)


def draw_hopping_block(key, part):
    key = jax.random.fold_in(key, 202)
    key_diag, key_off = jax.random.split(key)
    spread = 0.3 / jnp.sqrt(ORBITALS * 1.0)
    diagonal = jax.random.uniform(key_diag, (ORBITALS,), jnp.float32, 0.8, 1.2)
    rough = jnp.clip(jax.random.normal(key_off, (ORBITALS, ORBITALS), jnp.float32), -4.0, 4.0)
    return spread * rough + jnp.diag(diagonal)


def draw_phonon_shift(key, part):
    key = jax.random.fold_in(key, 303)
    key_values, key_order = jax.random.split(key)
    values = jax.random.randint(key_values, (PHONON_MODES,), 1, ENERGY_DEV + 1, dtype=jnp.int32)
    order = jax.random.permutation(key_order, PHONON_MODES)
    values = values.at[order[0]].set(ENERGY_DEV)
    return values.at[order[1]].set(1)


def place_ends(array, key, least, top_value):
    index_at = [jax.random.randint(jax.random.fold_in(key, axis), (), 0, length) for axis, length in enumerate(array.shape)]
    main_axis = array.shape.index(max(array.shape))
    beside = index_at[:main_axis] + [(index_at[main_axis] + 1) % array.shape[main_axis]] + index_at[main_axis + 1:]
    return array.at[tuple(index_at)].set(least).at[tuple(beside)].set(top_value)


def block_levels(stream_key, shape, shards, least, top_value):
    loudness = 1.0
    for axis_at, shards_of in shards:
        heights = jax.random.uniform(jax.random.fold_in(jax.random.fold_in(stream_key, 6), axis_at), (shards_of,), jnp.float32, least / len(shards), top_value / len(shards))
        loudness = loudness * jnp.repeat(jnp.exp(heights), shape[axis_at] // shards_of).reshape((-1,) + (1,) * (len(shape) - 1 - axis_at))
    return loudness


def scatter_about(own_key, shape, scale, bound, cuts=(), kind=jnp.bfloat16):
    factor_of = block_levels(own_key, shape, cuts, -0.22, 0.18) if cuts else 1.0
    entries = jax.random.normal(own_key, shape, jnp.float32) * scale * factor_of
    return jnp.minimum(jnp.maximum(entries, -bound), bound).astype(kind)


def setup_inputs(seed: int = 0) -> dict:
    seeds = jax.random.split(jax.random.key(seed), 9)
    source = scatter_about(seeds[0], (SLABS, 2, ENERGIES, ORBITALS, COLUMNS), 0.2, 1.2, ((0, 8), (2, 4)), jnp.float32)
    onsite_block = draw_onsite_block(jax.random.fold_in(seeds[8], 71), 0)
    hopping_block = draw_hopping_block(jax.random.fold_in(seeds[8], 71), 0)
    potential_table = jnp.clip(jax.random.uniform(seeds[3], (LEVELS, ORBITALS), jnp.float32, -0.5, 0.5), -0.5, 0.5)
    slab_profile = place_ends(jax.random.randint(seeds[4], (SLABS,), 0, LEVELS), jax.random.fold_in(seeds[4], 1), 0, LEVELS - 1).astype(jnp.int32)
    occupation = jnp.clip(jnp.exp(math.log(1.0) - 2.3025851 * jax.random.uniform(seeds[5], (SLABS, ENERGIES, ORBITALS), jnp.float32) ** block_levels(seeds[5], (SLABS, ENERGIES, ORBITALS), ((0, 8), (1, 4)), -0.2, 0.2)), 0.1, 1.0)
    coupling = jnp.clip(jnp.exp(jax.random.uniform(seeds[6], (PHONON_MODES,), jnp.float32, math.log(0.02), math.log(0.08))), 0.02, 0.08)
    phonon_shift = draw_phonon_shift(jax.random.fold_in(seeds[8], 71), 0)
    return {"source": source, "onsite_block": onsite_block, "hopping_block": hopping_block, "potential_table": potential_table, "slab_profile": slab_profile, "occupation": occupation, "coupling": coupling, "phonon_shift": phonon_shift}


broadening = 0.05
energy_low = -1.2
energy_step = 0.15

def matmul_exact(left, right):
    return jnp.matmul(left, right, precision=lax.Precision.HIGHEST)

def complex_product(left, right):
    real = matmul_exact(left[..., 0, :, :], right[..., 0, :, :]) - matmul_exact(left[..., 1, :, :], right[..., 1, :, :])
    imag = matmul_exact(left[..., 0, :, :], right[..., 1, :, :]) + matmul_exact(left[..., 1, :, :], right[..., 0, :, :])
    return jnp.stack([real, imag], axis=-3)

def invert(block):
    real = block[..., 0, :, :]
    imag = block[..., 1, :, :]
    real = 0.5 * (real + jnp.swapaxes(real, -1, -2))
    imag = 0.5 * (imag + jnp.swapaxes(imag, -1, -2))
    lower_imag = jnp.linalg.cholesky(imag)
    weighed = jax.scipy.linalg.cho_solve((lower_imag, True), real)
    schur = imag + matmul_exact(real, weighed)
    schur = 0.5 * (schur + jnp.swapaxes(schur, -1, -2))
    lower_schur = jnp.linalg.cholesky(schur)
    identity = jnp.broadcast_to(jnp.eye(schur.shape[-1], dtype=schur.dtype), schur.shape)
    schur_inverse = jax.scipy.linalg.cho_solve((lower_schur, True), identity)
    return jnp.stack([matmul_exact(weighed, schur_inverse), -schur_inverse], axis=-3)

def reference(source, onsite_block, hopping_block, potential_table, slab_profile, occupation, coupling, phonon_shift):
    energy_total = occupation.shape[1]
    points = jnp.arange(energy_total, dtype=jnp.int32)
    weights = jnp.zeros((energy_total, energy_total), jnp.float32)
    for mode in range(PHONON_MODES):
        above = (points[None, :] == points[:, None] + phonon_shift[mode]).astype(jnp.float32)
        below = (points[None, :] == points[:, None] - phonon_shift[mode]).astype(jnp.float32)
        weights = weights + coupling[mode] * (above + below)
    damping = jnp.einsum('ek,skb->seb', weights, occupation, precision=lax.Precision.HIGHEST)
    chosen = (slab_profile[:, None] == jnp.arange(LEVELS, dtype=jnp.int32)[None, :]).astype(jnp.float32)
    potential = matmul_exact(chosen, potential_table)
    grid = energy_low + energy_step * points.astype(jnp.float32)
    identity = jnp.eye(ORBITALS, dtype=jnp.float32)
    hop_t = hopping_block.T

    def solve_energy(point):
        real_diag = grid[point] * identity - onsite_block - potential[:, :, None] * identity
        imag_diag = (broadening + damping[:, point])[:, :, None] * identity
        blocks = jnp.stack([real_diag, imag_diag], axis=1)
        right = source[:, :, point]

        def forward(carry, inputs):
            inverse, solved = carry
            block, rhs = inputs
            pivot = block - matmul_exact(hop_t, matmul_exact(inverse, hopping_block))
            rhs = rhs + matmul_exact(hop_t, solved)
            inverse = invert(pivot)
            solved = complex_product(inverse, rhs)
            return ((inverse, solved), (inverse, solved))
        start = (jnp.zeros((2, ORBITALS, ORBITALS), jnp.float32), jnp.zeros((2, ORBITALS, COLUMNS), jnp.float32))
        _, (inverses, solveds) = lax.scan(forward, start, (blocks, right))

        def backward(later, inputs):
            inverse, solved = inputs
            current = solved + complex_product(inverse, matmul_exact(hopping_block, later))
            return (current, current)
        _, result = lax.scan(backward, jnp.zeros((2, ORBITALS, COLUMNS), jnp.float32), (inverses, solveds), reverse=True)
        return result
    stacked = lax.map(solve_energy, points)
    amplitude = jnp.moveaxis(stacked, 0, 2)
    density = jnp.sum(amplitude[:, 0] ** 2 + amplitude[:, 1] ** 2, axis=-1)
    return (amplitude, density)
```

```python
import functools

import jax
import jax.numpy as jnp
from jax import lax
from jax.experimental import pallas as pl
from jax.experimental.pallas import tpu as pltpu
from jax.sharding import PartitionSpec as P

broadening = 0.05
energy_low = -1.2
energy_step = 0.15


def padded(block, sides, width):
    for axis, dim in sides:
        count = lax.axis_size(axis)
        forward = [(i, i + 1) for i in range(count - 1)]
        backward = [(target, source) for source, target in forward]
        low = lax.ppermute(
            lax.slice_in_dim(block, block.shape[dim] - width, None, axis=dim), axis, forward
        )
        high = lax.ppermute(lax.slice_in_dim(block, 0, width, axis=dim), axis, backward)
        block = jnp.concatenate([low, block, high], axis=dim)
    return block


def shifted(array, axis, by):
    count = lax.axis_size(axis)
    pairs = [(i, i + by) for i in range(count) if 0 <= i + by < count]
    return lax.ppermute(array, axis, pairs)


def swapped(array, axis):
    count = lax.axis_size(axis)
    return lax.ppermute(array, axis, [(i, i ^ 1) for i in range(count)])


def matmul_exact(left, right):
    return jnp.matmul(left, right, precision=lax.Precision.HIGHEST)


def complex_product(left, right):
    real = matmul_exact(left[0], right[0]) - matmul_exact(left[1], right[1])
    imag = matmul_exact(left[0], right[1]) + matmul_exact(left[1], right[0])
    return jnp.stack([real, imag], axis=0)


def turned(array):
    return jnp.swapaxes(array, -1, -2)


def halves(value):
    high = value.astype(jnp.bfloat16)
    return high, (value - high.astype(jnp.float32)).astype(jnp.bfloat16)


def dot_rows(left, right):
    return lax.dot_general(
        left, right, (((0,), (0,)), ((), ())), preferred_element_type=jnp.float32
    )


def complex_dot_rows(left_real, left_imag, right_real, right_imag):
    lrh, lrl = halves(left_real)
    lih, lil = halves(left_imag)
    rrh, rrl = halves(right_real)
    rih, ril = halves(right_imag)
    right = jnp.concatenate([rrh, rrl, rrh, rih, ril, rih], axis=0)
    for_real = jnp.concatenate([lrh, lrh, lrl, -lih, -lih, -lil], axis=0)
    for_imag = jnp.concatenate([lih, lih, lil, lrh, lrh, lrl], axis=0)
    return dot_rows(for_real, right), dot_rows(for_imag, right)


def invert_small(blocks):
    size = blocks[0][0].shape[0]
    lane = lax.broadcasted_iota(jnp.int32, (1, size), 1)
    row = lax.broadcasted_iota(jnp.int32, (size, 1), 0)
    for k in range(size):
        at_lane = lane == k
        at_row = row == k
        after = []
        for real, imag in blocks:
            col_real = real[:, k : k + 1]
            col_imag = imag[:, k : k + 1]
            pivot_real = col_real[k : k + 1]
            pivot_imag = col_imag[k : k + 1]
            scale = 1.0 / (pivot_real * pivot_real + pivot_imag * pivot_imag)
            inv_real = pivot_real * scale
            inv_imag = -pivot_imag * scale
            row_real = jnp.where(at_lane, 1.0, real[k : k + 1])
            row_imag = jnp.where(at_lane, 0.0, imag[k : k + 1])
            new_real = inv_real * row_real - inv_imag * row_imag
            new_imag = inv_real * row_imag + inv_imag * row_real
            real = jnp.where(at_lane, 0.0, real) - (col_real * new_real - col_imag * new_imag)
            imag = jnp.where(at_lane, 0.0, imag) - (col_real * new_imag + col_imag * new_real)
            real = jnp.where(at_row, new_real, real)
            imag = jnp.where(at_row, new_imag, imag)
            after.append((real, imag))
        blocks = after
    return blocks


def invert_steps(state, batch, size, block):
    width = state.shape[-1]

    def step(index, carry):
        low = pl.multiple_of(index * block, block)
        lane = lax.broadcasted_iota(jnp.int32, (block, width), 1)
        row = lax.broadcasted_iota(jnp.int32, (block, width), 0)
        inside = (lane >= low) & (lane < low + block)
        unit = jnp.where(lane == row + low, 1.0, 0.0)
        sign = jnp.where(lane < low, -1.0, 1.0)
        back = lax.rem(width - low, width)
        rows = []
        small = []
        for b in range(batch):
            real = state[b, 0, pl.ds(low, block), :]
            imag = state[b, 1, pl.ds(low, block), :]
            rows.append((real, imag))
            small.append(
                (
                    pltpu.roll(real, back, 1)[:, :block],
                    pltpu.roll(imag, back, 1)[:, :block],
                )
            )
        small = invert_small(small)
        all_lane = lax.broadcasted_iota(jnp.int32, (size, width), 1)
        all_inside = (all_lane >= low) & (all_lane < low + block)
        for b in range(batch):
            real, imag = rows[b]
            new_real, new_imag = complex_dot_rows(
                *small[b], jnp.where(inside, unit, real), jnp.where(inside, 0.0, imag)
            )
            change_real, change_imag = complex_dot_rows(
                (sign * real)[:, :size], (sign * imag)[:, :size], new_real, new_imag
            )
            state[b, 0] = jnp.where(all_inside, 0.0, state[b, 0]) - change_real
            state[b, 1] = jnp.where(all_inside, 0.0, state[b, 1]) - change_imag
            state[b, 0, pl.ds(low, block), :] = new_real
            state[b, 1, pl.ds(low, block), :] = new_imag
        return carry

    lax.fori_loop(0, size // block, step, 0)


def invert_kernel(block, p_ref, g_ref, state):
    batch, size = p_ref.shape[1], p_ref.shape[-1]
    state[...] = jnp.zeros_like(state)
    for b in range(batch):
        for part in range(2):
            value = p_ref[part, b]
            state[b, part, :, :size] = 0.5 * (value + value.T)
    invert_steps(state, batch, size, block)
    for b in range(batch):
        for part in range(2):
            g_ref[part, b] = state[b, part, :, :size]


def invert(block):
    batch, size = block.shape[1], block.shape[-1]
    step = next(s for s in (32, 16, 8, 1) if size % s == 0)
    width = -(-size // 128) * 128
    return pl.pallas_call(
        functools.partial(invert_kernel, step),
        out_shape=jax.ShapeDtypeStruct(block.shape, jnp.float32),
        in_specs=[pl.BlockSpec(memory_space=pltpu.VMEM)],
        out_specs=pl.BlockSpec(memory_space=pltpu.VMEM),
        scratch_shapes=[pltpu.VMEM((batch, 2, size, width), jnp.float32)],
        compiler_params=pltpu.CompilerParams(vmem_limit_bytes=32 * 1024 * 1024),
    )(block)


def per_device(
    source,
    onsite_block,
    hopping_block,
    potential_table,
    slab_profile,
    occupation,
    coupling,
    phonon_shift,
):
    slab_count = occupation.shape[0]
    energy_count = occupation.shape[1]
    orbitals = onsite_block.shape[0]
    half = energy_count // 2
    if slab_count != 2 or energy_count % 2 or lax.axis_size("slab") % 2:
        raise ValueError("unsupported shape")
    hop = hopping_block
    hop_t = hopping_block.T
    place = lax.axis_index("slab")
    upper_half = (place % 2) == 1
    widened = padded(occupation, (("energy", 1),), energy_count)
    own_points = jnp.arange(energy_count, dtype=jnp.int32)[:, None]
    all_points = jnp.arange(3 * energy_count, dtype=jnp.int32)[None, :]
    weights = jnp.zeros((energy_count, 3 * energy_count), jnp.float32)
    for mode in range(phonon_shift.shape[0]):
        above = (all_points == own_points + energy_count + phonon_shift[mode]).astype(jnp.float32)
        below = (all_points == own_points + energy_count - phonon_shift[mode]).astype(jnp.float32)
        weights = weights + coupling[mode] * (above + below)
    damping = jnp.einsum("ek,skb->seb", weights, widened, precision=lax.Precision.HIGHEST)
    chosen = (
        slab_profile[:, None] == jnp.arange(potential_table.shape[0], dtype=jnp.int32)[None, :]
    ).astype(jnp.float32)
    potential = matmul_exact(chosen, potential_table)

    def exchanged(array, axis):
        low = lax.slice_in_dim(array, 0, half, axis=axis)
        high = lax.slice_in_dim(array, half, energy_count, axis=axis)
        kept = jnp.where(upper_half, high, low)
        other = swapped(jnp.where(upper_half, low, high), "slab")
        return kept, other

    def ordered(kept, other):
        return jnp.where(
            upper_half,
            jnp.concatenate([other, kept], axis=0),
            jnp.concatenate([kept, other], axis=0),
        )

    shared = jnp.concatenate(
        [damping, jnp.broadcast_to(potential[:, None], damping.shape)], axis=-1
    )
    shared = ordered(*exchanged(shared, 1))
    damping = shared[..., :orbitals]
    potential = shared[..., orbitals:]
    right = ordered(*exchanged(source, 2))

    first_point = lax.axis_index("energy") * energy_count + jnp.where(upper_half, half, 0)
    energies = energy_low + energy_step * (
        first_point + jnp.arange(half, dtype=jnp.int32)
    ).astype(jnp.float32)
    identity = jnp.eye(orbitals, dtype=jnp.float32)
    real_diag = (
        energies[None, :, None, None] * identity - onsite_block - potential[..., None] * identity
    )
    imag_diag = (broadening + damping)[..., None] * identity
    blocks = jnp.stack([real_diag, imag_diag], axis=1)

    pair = invert(jnp.concatenate([blocks[0], blocks[2]], axis=1))
    g0, g2 = pair[:, :half], pair[:, half:]
    both = jnp.concatenate([hop, hop_t], axis=-1)
    g0h = matmul_exact(g0, both)
    g2h = matmul_exact(g2, both)
    g0_hop, g0_hop_t = g0h[..., :orbitals], g0h[..., orbitals:]
    g2_hop, g2_hop_t = g2h[..., :orbitals], g2h[..., orbitals:]
    pivot = blocks[1] - matmul_exact(hop_t, g0_hop) - matmul_exact(hop, g2_hop_t)
    g1 = invert(pivot)
    from_below = -matmul_exact(hop_t, g0_hop_t)
    from_above = -matmul_exact(hop, g2_hop)
    b0, b1, b2, b3 = right[0], right[1], right[2], right[3]
    z0 = complex_product(g0, b0)
    z2 = complex_product(g2, b2)
    b1 = b1 + matmul_exact(hop_t, z0) + matmul_exact(hop, z2)
    scaled = complex_product(g1, jnp.concatenate([from_below, from_above, b1], axis=-1))
    s_below = scaled[..., :orbitals]
    s_above = scaled[..., orbitals : 2 * orbitals]
    z1 = scaled[..., 2 * orbitals :]
    outward = complex_product(turned(from_below), scaled)
    inward = complex_product(
        turned(from_above), jnp.concatenate([s_below, s_above, z1], axis=-1)
    )
    lower = -inward[..., :orbitals]
    own_block = blocks[3] - matmul_exact(hop_t, g2_hop) - inward[..., orbitals : 2 * orbitals]
    own_right = b3 + matmul_exact(hop_t, z2) - inward[..., 2 * orbitals :]
    outgoing = jnp.concatenate(
        [
            -matmul_exact(hop, g0_hop_t) - outward[..., :orbitals],
            -outward[..., orbitals : 2 * orbitals],
            matmul_exact(hop, z0) - outward[..., 2 * orbitals :],
        ],
        axis=-1,
    )
    incoming = shifted(outgoing, "slab", -2)
    pivot_now = own_block + incoming[..., :orbitals]
    upper_now = incoming[..., orbitals : 2 * orbitals]
    right_now = own_right + incoming[..., 2 * orbitals :]
    lower_now = lower
    count = lax.axis_size("slab") // 2
    for level in range((count - 1).bit_length()):
        distance = 1 << level
        last = 2 * distance >= count
        scaled = complex_product(
            invert(pivot_now), jnp.concatenate([lower_now, right_now, upper_now], axis=-1)
        )
        split = orbitals + right_now.shape[-1]
        if last:
            below = shifted(scaled[..., orbitals:], "slab", 2 * distance)
            above = shifted(scaled[..., :split], "slab", -2 * distance)
            product_low = complex_product(lower_now, below)
            product_up = complex_product(upper_now, above)
            pivot_now = (
                pivot_now - product_low[..., split - orbitals :] - product_up[..., :orbitals]
            )
            right_now = (
                right_now - product_low[..., : split - orbitals] - product_up[..., orbitals:]
            )
        else:
            below = shifted(scaled, "slab", 2 * distance)
            above = shifted(scaled, "slab", -2 * distance)
            product_low = complex_product(lower_now, below)
            product_up = complex_product(upper_now, above)
            pivot_now = pivot_now - product_low[..., split:] - product_up[..., :orbitals]
            right_now = (
                right_now - product_low[..., orbitals:split] - product_up[..., orbitals:split]
            )
            lower_now = -product_low[..., :orbitals]
            upper_now = -product_up[..., split:]
    x3 = complex_product(invert(pivot_now), right_now)
    previous = shifted(x3, "slab", 2)
    x1 = z1 - complex_product(s_below, previous) - complex_product(s_above, x3)
    x0 = z0 + complex_product(g0, matmul_exact(hop_t, previous) + matmul_exact(hop, x1))
    x2 = z2 + complex_product(g2, matmul_exact(hop_t, x1) + matmul_exact(hop, x3))
    result = jnp.stack([x0, x1, x2, x3], axis=0)
    kept = jnp.where(upper_half, result[2:], result[:2])
    other = swapped(jnp.where(upper_half, result[:2], result[2:]), "slab")
    amplitude = jnp.where(
        upper_half,
        jnp.concatenate([other, kept], axis=2),
        jnp.concatenate([kept, other], axis=2),
    )
    density = jnp.sum(amplitude[:, 0] ** 2 + amplitude[:, 1] ** 2, axis=-1)
    return (amplitude, density)


def solution(mesh):
    placed = (
        P("slab", None, "energy", None, None),
        P(),
        P(),
        P(),
        P("slab"),
        P("slab", "energy", None),
        P(),
        P(),
    )
    return jax.shard_map(
        per_device,
        mesh=mesh,
        in_specs=placed,
        out_specs=(P("slab", None, "energy", None, None), P("slab", "energy", None)),
        check_vma=False,
    )
```

```python
import functools

import jax
import jax.numpy as jnp
from jax import lax
from jax.experimental import pallas as pl
from jax.experimental.pallas import tpu as pltpu
from jax.sharding import PartitionSpec as P

broadening = 0.05
energy_low = -1.2
energy_step = 0.15


def padded(block, sides, width):
    for axis, dim in sides:
        count = lax.axis_size(axis)
        forward = [(i, i + 1) for i in range(count - 1)]
        backward = [(target, source) for source, target in forward]
        low = lax.ppermute(
            lax.slice_in_dim(block, block.shape[dim] - width, None, axis=dim), axis, forward
        )
        high = lax.ppermute(lax.slice_in_dim(block, 0, width, axis=dim), axis, backward)
        block = jnp.concatenate([low, block, high], axis=dim)
    return block


def shifted(array, axis, by):
    count = lax.axis_size(axis)
    pairs = [(i, i + by) for i in range(count) if 0 <= i + by < count]
    return lax.ppermute(array, axis, pairs)


def swapped(array, axis):
    count = lax.axis_size(axis)
    return lax.ppermute(array, axis, [(i, i ^ 1) for i in range(count)])


def matmul_exact(left, right):
    return jnp.matmul(left, right, precision=lax.Precision.HIGHEST)


def halves(value):
    high = value.astype(jnp.bfloat16)
    return high, (value - high.astype(jnp.float32)).astype(jnp.bfloat16)


def dot_rows(left, right):
    return lax.dot_general(
        left, right, (((0,), (0,)), ((), ())), preferred_element_type=jnp.float32
    )


def complex_dot_rows(left_real, left_imag, right_real, right_imag):
    lrh, lrl = halves(left_real)
    lih, lil = halves(left_imag)
    rrh, rrl = halves(right_real)
    rih, ril = halves(right_imag)
    right = jnp.concatenate([rrh, rrl, rrh, rih, ril, rih], axis=0)
    for_real = jnp.concatenate([lrh, lrh, lrl, -lih, -lih, -lil], axis=0)
    for_imag = jnp.concatenate([lih, lih, lil, lrh, lrh, lrl], axis=0)
    return dot_rows(for_real, right), dot_rows(for_imag, right)


def dot_split(left, right):
    lh, ll = left
    rh, rl = right
    dot = functools.partial(jnp.dot, preferred_element_type=jnp.float32)
    return dot(lh, rh) + (dot(lh, rl) + dot(ll, rh))


def real_dot(left, right):
    split = halves(left)
    return tuple(dot_split(split, halves(part)) for part in right)


def dot_real(left, right):
    split = halves(right)
    return tuple(dot_split(halves(part), split) for part in left)


def complex_dot(left, right):
    lr, li = halves(left[0]), halves(left[1])
    rr, ri = halves(right[0]), halves(right[1])
    return (
        dot_split(lr, rr) - dot_split(li, ri),
        dot_split(lr, ri) + dot_split(li, rr),
    )


def plus(left, right):
    return left[0] + right[0], left[1] + right[1]


def minus(left, right):
    return left[0] - right[0], left[1] - right[1]


def negative(value):
    return -value[0], -value[1]


def turned(value):
    return value[0].T, value[1].T


def take(ref, *index):
    return ref[(0,) + index], ref[(1,) + index]


def put(ref, value, *index):
    ref[(0,) + index] = value[0]
    ref[(1,) + index] = value[1]


def invert_small(blocks):
    size = blocks[0][0].shape[0]
    panel = 4 if size % 4 == 0 else 1
    lane = lax.broadcasted_iota(jnp.int32, (1, size), 1)
    row = lax.broadcasted_iota(jnp.int32, (size, 1), 0)
    for start in range(0, size, panel):
        spread = [
            [
                tuple(
                    jnp.broadcast_to(part[:, k : k + 1], (size, size)) for part in parts
                )
                for k in range(start, start + panel)
            ]
            for parts in blocks
        ]
        for at in range(panel):
            k = start + at
            at_lane = lane == k
            at_row = row == k
            after = []
            for (real, imag), columns in zip(blocks, spread):
                col_real, col_imag = columns[at]
                pivot_real = col_real[k : k + 1]
                pivot_imag = col_imag[k : k + 1]
                scale = 1.0 / (pivot_real * pivot_real + pivot_imag * pivot_imag)
                inv_real = pivot_real * scale
                inv_imag = -pivot_imag * scale
                for later in range(at + 1, panel):
                    j = start + later
                    entry_real = col_real[j : j + 1]
                    entry_imag = col_imag[j : j + 1]
                    new_real = inv_real * entry_real - inv_imag * entry_imag
                    new_imag = inv_real * entry_imag + inv_imag * entry_real
                    old_real, old_imag = columns[later]
                    columns[later] = (
                        jnp.where(
                            at_row,
                            new_real,
                            old_real - (col_real * new_real - col_imag * new_imag),
                        ),
                        jnp.where(
                            at_row,
                            new_imag,
                            old_imag - (col_real * new_imag + col_imag * new_real),
                        ),
                    )
                row_real = jnp.where(at_lane, 1.0, real[k : k + 1])
                row_imag = jnp.where(at_lane, 0.0, imag[k : k + 1])
                new_real = inv_real * row_real - inv_imag * row_imag
                new_imag = inv_real * row_imag + inv_imag * row_real
                real = jnp.where(at_lane, 0.0, real) - (col_real * new_real - col_imag * new_imag)
                imag = jnp.where(at_lane, 0.0, imag) - (col_real * new_imag + col_imag * new_real)
                real = jnp.where(at_row, new_real, real)
                imag = jnp.where(at_row, new_imag, imag)
                after.append((real, imag))
            blocks = after
    return blocks


def invert_steps(state, batch, size):
    width = state.shape[-1]
    block = next(s for s in (32, 16, 8, 1) if size % s == 0)

    def step(index, carry):
        low = pl.multiple_of(index * block, block)
        lane = lax.broadcasted_iota(jnp.int32, (block, width), 1)
        row = lax.broadcasted_iota(jnp.int32, (block, width), 0)
        inside = (lane >= low) & (lane < low + block)
        unit = jnp.where(lane == row + low, 1.0, 0.0)
        sign = jnp.where(lane < low, -1.0, 1.0)
        back = lax.rem(width - low, width)
        rows = []
        small = []
        for b in range(batch):
            real = state[b, 0, pl.ds(low, block), :]
            imag = state[b, 1, pl.ds(low, block), :]
            rows.append((real, imag))
            small.append(
                (
                    pltpu.roll(real, back, 1)[:, :block],
                    pltpu.roll(imag, back, 1)[:, :block],
                )
            )
        small = invert_small(small)
        all_lane = lax.broadcasted_iota(jnp.int32, (size, width), 1)
        all_inside = (all_lane >= low) & (all_lane < low + block)
        for b in range(batch):
            real, imag = rows[b]
            new_real, new_imag = complex_dot_rows(
                *small[b], jnp.where(inside, unit, real), jnp.where(inside, 0.0, imag)
            )
            change_real, change_imag = complex_dot_rows(
                (sign * real)[:, :size], (sign * imag)[:, :size], new_real, new_imag
            )
            state[b, 0] = jnp.where(all_inside, 0.0, state[b, 0]) - change_real
            state[b, 1] = jnp.where(all_inside, 0.0, state[b, 1]) - change_imag
            state[b, 0, pl.ds(low, block), :] = new_real
            state[b, 1, pl.ds(low, block), :] = new_imag
        return carry

    lax.fori_loop(0, size // block, step, 0)


def invert_all(state, blocks):
    size = blocks[0][0].shape[0]
    for b, parts in enumerate(blocks):
        for part in range(2):
            state[b, part, :, :size] = 0.5 * (parts[part] + parts[part].T)
            if state.shape[-1] > size:
                state[b, part, :, size:] = jnp.zeros(
                    (size, state.shape[-1] - size), jnp.float32
                )
    invert_steps(state, len(blocks), size)
    return [(state[b, 0, :, :size], state[b, 1, :, :size]) for b in range(len(blocks))]


def run(kernel, out_shapes, inputs, size=0, batch=0, micros=2):
    scratch = []
    if batch:
        scratch = [pltpu.VMEM((batch, 2, size, -(-size // 128) * 128), jnp.float32)]
    return pl.pallas_call(
        kernel,
        out_shape=[jax.ShapeDtypeStruct(shape, jnp.float32) for shape in out_shapes],
        in_specs=[pl.BlockSpec(memory_space=pltpu.VMEM)] * len(inputs),
        out_specs=[pl.BlockSpec(memory_space=pltpu.VMEM)] * len(out_shapes),
        scratch_shapes=scratch,
        compiler_params=pltpu.CompilerParams(vmem_limit_bytes=48 * 1024 * 1024),
        cost_estimate=pl.CostEstimate(
            flops=micros * 1000000000, bytes_accessed=1000000, transcendentals=0
        ),
    )(*inputs)


def local_kernel(
    onsite_ref, hop_ref, real_ref, imag_ref,
    g0_ref, g1_ref, g2_ref, below_ref, above_ref, sb_ref, sa_ref,
    out_pivot_ref, out_upper_ref, pivot_ref, lower_ref, state,
):
    count = real_ref.shape[1]
    size = onsite_ref.shape[0]
    eye = lax.broadcasted_iota(jnp.int32, (size, size), 0) == lax.broadcasted_iota(
        jnp.int32, (size, size), 1
    )
    hop = hop_ref[...]
    hop_t = hop.T

    def block(slab, e):
        return (
            jnp.where(eye, real_ref[slab, e : e + 1, :], 0.0) - onsite_ref[...],
            jnp.where(eye, imag_ref[slab, e : e + 1, :], 0.0),
        )

    pairs = invert_all(
        state, [block(0, e) for e in range(count)] + [block(2, e) for e in range(count)]
    )
    middle = []
    for e in range(count):
        g0, g2 = pairs[e], pairs[count + e]
        put(g0_ref, g0, e)
        put(g2_ref, g2, e)
        g0h, g0t = dot_real(g0, hop), dot_real(g0, hop_t)
        g2h, g2t = dot_real(g2, hop), dot_real(g2, hop_t)
        put(below_ref, negative(real_dot(hop_t, g0t)), e)
        put(above_ref, negative(real_dot(hop, g2h)), e)
        put(out_pivot_ref, negative(real_dot(hop, g0t)), e)
        put(pivot_ref, minus(block(3, e), real_dot(hop_t, g2h)), e)
        middle.append(minus(block(1, e), plus(real_dot(hop_t, g0h), real_dot(hop, g2t))))
    for e, g1 in enumerate(invert_all(state, middle)):
        put(g1_ref, g1, e)
        below, above = take(below_ref, e), take(above_ref, e)
        below_t, above_t = turned(below), turned(above)
        sb = complex_dot(g1, below)
        sa = complex_dot(g1, above)
        put(sb_ref, sb, e)
        put(sa_ref, sa, e)
        put(out_pivot_ref, minus(take(out_pivot_ref, e), complex_dot(below_t, sb)), e)
        put(pivot_ref, minus(take(pivot_ref, e), complex_dot(above_t, sa)), e)
        lower = negative(complex_dot(above_t, sb))
        put(lower_ref, lower, e)
        put(out_upper_ref, turned(lower), e)


def local_right_kernel(
    hop_ref, g0_ref, g1_ref, g2_ref, below_ref, above_ref, right_ref,
    z0_ref, z1_ref, z2_ref, out_ref, own_ref,
):
    hop = hop_ref[...]
    hop_t = hop.T
    for e in range(g0_ref.shape[1]):
        b0, b1, b2, b3 = (
            (right_ref[slab, 0, e], right_ref[slab, 1, e]) for slab in range(4)
        )
        z0 = complex_dot(take(g0_ref, e), b0)
        z2 = complex_dot(take(g2_ref, e), b2)
        b1 = plus(b1, plus(real_dot(hop_t, z0), real_dot(hop, z2)))
        z1 = complex_dot(take(g1_ref, e), b1)
        put(z0_ref, z0, e)
        put(z1_ref, z1, e)
        put(z2_ref, z2, e)
        put(
            out_ref,
            minus(real_dot(hop, z0), complex_dot(turned(take(below_ref, e)), z1)),
            e,
        )
        put(
            own_ref,
            minus(
                plus(b3, real_dot(hop_t, z2)), complex_dot(turned(take(above_ref, e)), z1)
            ),
            e,
        )


def first_kernel(own_ref, more_ref, pivot_ref, g_ref, state):
    count = own_ref.shape[1]
    for e in range(count):
        put(pivot_ref, plus(take(own_ref, e), take(more_ref, e)), e)
    inverse = invert_all(state, [take(pivot_ref, e) for e in range(count)])
    for e in range(count):
        put(g_ref, inverse[e], e)


def level_kernel(old_ref, lower_ref, upper_ref, below_ref, above_ref, pivot_ref, g_ref, state):
    count = old_ref.shape[1]
    for e in range(count):
        change = plus(
            complex_dot(take(lower_ref, e), take(below_ref, e)),
            complex_dot(take(upper_ref, e), take(above_ref, e)),
        )
        put(pivot_ref, minus(take(old_ref, e), change), e)
    inverse = invert_all(state, [take(pivot_ref, e) for e in range(count)])
    for e in range(count):
        put(g_ref, inverse[e], e)


def scale_kernel(g_ref, lower_ref, upper_ref, xl_ref, xu_ref):
    for e in range(g_ref.shape[1]):
        g = take(g_ref, e)
        put(xl_ref, complex_dot(g, take(lower_ref, e)), e)
        put(xu_ref, complex_dot(g, take(upper_ref, e)), e)


def product_kernel(left_ref, right_ref, out_ref):
    for e in range(left_ref.shape[1]):
        put(out_ref, complex_dot(take(left_ref, e), take(right_ref, e)), e)


def coupling_kernel(lower_ref, upper_ref, below_ref, above_ref, new_lower_ref, new_upper_ref):
    for e in range(lower_ref.shape[1]):
        put(new_lower_ref, negative(complex_dot(take(lower_ref, e), take(below_ref, e))), e)
        put(new_upper_ref, negative(complex_dot(take(upper_ref, e), take(above_ref, e))), e)


def right_kernel(
    g_ref, lower_ref, upper_ref, below_ref, above_ref, right_ref, new_ref, x_ref
):
    for e in range(lower_ref.shape[1]):
        change = plus(
            complex_dot(take(lower_ref, e), take(below_ref, e)),
            complex_dot(take(upper_ref, e), take(above_ref, e)),
        )
        new = minus(take(right_ref, e), change)
        put(new_ref, new, e)
        put(x_ref, complex_dot(take(g_ref, e), new), e)


def middle_kernel(z1_ref, sb_ref, sa_ref, previous_ref, x3_ref, x1_ref):
    for e in range(z1_ref.shape[1]):
        change = plus(
            complex_dot(take(sb_ref, e), take(previous_ref, e)),
            complex_dot(take(sa_ref, e), take(x3_ref, e)),
        )
        put(x1_ref, minus(take(z1_ref, e), change), e)


def outer_kernel(
    hop_ref, g0_ref, g2_ref, z0_ref, z2_ref, previous_ref, x1_ref, x3_ref, x0_ref, x2_ref
):
    hop = hop_ref[...]
    hop_t = hop.T
    for e in range(z0_ref.shape[1]):
        x1 = take(x1_ref, e)
        for_0 = plus(real_dot(hop_t, take(previous_ref, e)), real_dot(hop, x1))
        for_2 = plus(real_dot(hop_t, x1), real_dot(hop, take(x3_ref, e)))
        put(x0_ref, plus(take(z0_ref, e), complex_dot(take(g0_ref, e), for_0)), e)
        put(x2_ref, plus(take(z2_ref, e), complex_dot(take(g2_ref, e), for_2)), e)


def per_device(
    source,
    onsite_block,
    hopping_block,
    potential_table,
    slab_profile,
    occupation,
    coupling,
    phonon_shift,
):
    slab_count = occupation.shape[0]
    energy_count = occupation.shape[1]
    orbitals = onsite_block.shape[0]
    half = energy_count // 2
    if slab_count != 2 or energy_count % 2 or lax.axis_size("slab") % 2:
        raise ValueError("unsupported shape")
    hop = hopping_block
    place = lax.axis_index("slab")
    upper_half = (place % 2) == 1
    widened = padded(occupation, (("energy", 1),), energy_count)
    own_points = jnp.arange(energy_count, dtype=jnp.int32)[:, None]
    all_points = jnp.arange(3 * energy_count, dtype=jnp.int32)[None, :]
    weights = jnp.zeros((energy_count, 3 * energy_count), jnp.float32)
    for mode in range(phonon_shift.shape[0]):
        above = (all_points == own_points + energy_count + phonon_shift[mode]).astype(jnp.float32)
        below = (all_points == own_points + energy_count - phonon_shift[mode]).astype(jnp.float32)
        weights = weights + coupling[mode] * (above + below)
    damping = jnp.einsum("ek,skb->seb", weights, widened, precision=lax.Precision.HIGHEST)
    chosen = (
        slab_profile[:, None] == jnp.arange(potential_table.shape[0], dtype=jnp.int32)[None, :]
    ).astype(jnp.float32)
    potential = matmul_exact(chosen, potential_table)

    def exchanged(array, axis):
        low = lax.slice_in_dim(array, 0, half, axis=axis)
        high = lax.slice_in_dim(array, half, energy_count, axis=axis)
        kept = jnp.where(upper_half, high, low)
        other = swapped(jnp.where(upper_half, low, high), "slab")
        return kept, other

    def ordered(kept, other):
        return jnp.where(
            upper_half,
            jnp.concatenate([other, kept], axis=0),
            jnp.concatenate([kept, other], axis=0),
        )

    shared = jnp.concatenate(
        [damping, jnp.broadcast_to(potential[:, None], damping.shape)], axis=-1
    )
    shared = ordered(*exchanged(shared, 1))
    damping = shared[..., :orbitals]
    potential = shared[..., orbitals:]
    right = ordered(*exchanged(source, 2))

    first_point = lax.axis_index("energy") * energy_count + jnp.where(upper_half, half, 0)
    energies = energy_low + energy_step * (
        first_point + jnp.arange(half, dtype=jnp.int32)
    ).astype(jnp.float32)
    real_diag = energies[None, :, None] - potential
    imag_diag = broadening + damping
    square = (2, half, orbitals, orbitals)
    tall = (2, half, orbitals, source.shape[-1])
    g0, g1, g2, below, above, sb, sa, out_pivot, out_upper, pivot, lower = run(
        local_kernel,
        [square] * 11,
        [onsite_block, hop, real_diag, imag_diag],
        orbitals,
        2 * half,
        30,
    )
    more = shifted(out_pivot, "slab", -2)
    z0, z1, z2, out_right, right_now = run(
        local_right_kernel, [tall] * 5, [hop, g0, g1, g2, below, above, right]
    )
    upper = shifted(out_upper, "slab", -2)
    right_now = (right_now, shifted(out_right, "slab", -2))
    count = lax.axis_size("slab") // 2
    pivot, inverse = run(first_kernel, [square] * 2, [pivot, more], orbitals, half, 14)
    right_now = right_now[0] + right_now[1]
    scaled_right = None
    for level in range((count - 1).bit_length()):
        distance = 2 << level
        last = distance >= count
        x_lower, x_upper = run(scale_kernel, [square] * 2, [inverse, lower, upper])
        below_upper = shifted(x_upper, "slab", distance)
        above_lower = shifted(x_lower, "slab", -distance)
        if scaled_right is None:
            (scaled_right,) = run(product_kernel, [tall], [inverse, right_now])
        if not last:
            below_lower = shifted(x_lower, "slab", distance)
            above_upper = shifted(x_upper, "slab", -distance)
        below_right = shifted(scaled_right, "slab", distance)
        above_right = shifted(scaled_right, "slab", -distance)
        pivot, inverse = run(
            level_kernel,
            [square] * 2,
            [pivot, lower, upper, below_upper, above_lower],
            orbitals,
            half,
            14,
        )
        right_now, scaled_right = run(
            right_kernel,
            [tall] * 2,
            [inverse, lower, upper, below_right, above_right, right_now],
        )
        if not last:
            lower, upper = run(
                coupling_kernel, [square] * 2, [lower, upper, below_lower, above_upper]
            )
    if scaled_right is None:
        (scaled_right,) = run(product_kernel, [tall], [inverse, right_now])
    x3 = scaled_right
    previous = shifted(x3, "slab", 2)
    (x1,) = run(middle_kernel, [tall], [z1, sb, sa, previous, x3])
    first = swapped(jnp.where(upper_half, x1, x3), "slab")
    x0, x2 = run(outer_kernel, [tall] * 2, [hop, g0, g2, z0, z2, previous, x1, x3])
    second = swapped(jnp.where(upper_half, x0, x2), "slab")
    kept = jnp.where(upper_half, jnp.stack([x2, x3]), jnp.stack([x0, x1]))
    other = jnp.stack([second, first])
    amplitude = jnp.where(
        upper_half,
        jnp.concatenate([other, kept], axis=2),
        jnp.concatenate([kept, other], axis=2),
    )
    density = jnp.sum(amplitude[:, 0] ** 2 + amplitude[:, 1] ** 2, axis=-1)
    return (amplitude, density)


def solution(mesh):
    placed = (
        P("slab", None, "energy", None, None),
        P(),
        P(),
        P(),
        P("slab"),
        P("slab", "energy", None),
        P(),
        P(),
    )
    return jax.shard_map(
        per_device,
        mesh=mesh,
        in_specs=placed,
        out_specs=(P("slab", None, "energy", None, None), P("slab", "energy", None)),
        check_vma=False,
    )
```

```python
import functools

import jax
import jax.numpy as jnp
from jax import lax
from jax.experimental import pallas as pl
from jax.experimental.pallas import tpu as pltpu
from jax.sharding import PartitionSpec as P

broadening = 0.05
energy_low = -1.2
energy_step = 0.15


def padded(block, sides, width):
    for axis, dim in sides:
        count = lax.axis_size(axis)
        forward = [(i, i + 1) for i in range(count - 1)]
        backward = [(target, source) for source, target in forward]
        low = lax.ppermute(
            lax.slice_in_dim(block, block.shape[dim] - width, None, axis=dim), axis, forward
        )
        high = lax.ppermute(lax.slice_in_dim(block, 0, width, axis=dim), axis, backward)
        block = jnp.concatenate([low, block, high], axis=dim)
    return block


def shifted(array, axis, by):
    count = lax.axis_size(axis)
    pairs = [(i, i + by) for i in range(count) if 0 <= i + by < count]
    return lax.ppermute(array, axis, pairs)


def swapped(array, axis):
    count = lax.axis_size(axis)
    return lax.ppermute(array, axis, [(i, i ^ 1) for i in range(count)])


def halves(value):
    high = value.astype(jnp.bfloat16)
    return high, (value - high.astype(jnp.float32)).astype(jnp.bfloat16)


def dot_rows(left, right):
    return lax.dot_general(
        left, right, (((0,), (0,)), ((), ())), preferred_element_type=jnp.float32
    )


def complex_dot_rows(left_real, left_imag, right_real, right_imag):
    lrh, lrl = halves(left_real)
    lih, lil = halves(left_imag)
    rrh, rrl = halves(right_real)
    rih, ril = halves(right_imag)
    right = jnp.concatenate([rrh, rrl, rrh, rih, ril, rih], axis=0)
    for_real = jnp.concatenate([lrh, lrh, lrl, -lih, -lih, -lil], axis=0)
    for_imag = jnp.concatenate([lih, lih, lil, lrh, lrh, lrl], axis=0)
    return dot_rows(for_real, right), dot_rows(for_imag, right)


def dot_split(left, right):
    lh, ll = left
    rh, rl = right
    dot = functools.partial(jnp.dot, preferred_element_type=jnp.float32)
    return dot(lh, rh) + (dot(lh, rl) + dot(ll, rh))


def real_dot(left, right):
    split = halves(left)
    return tuple(dot_split(split, halves(part)) for part in right)


def dot_real(left, right):
    split = halves(right)
    return tuple(dot_split(halves(part), split) for part in left)


def complex_dot(left, right):
    lr, li = halves(left[0]), halves(left[1])
    rr, ri = halves(right[0]), halves(right[1])
    return (
        dot_split(lr, rr) - dot_split(li, ri),
        dot_split(lr, ri) + dot_split(li, rr),
    )


def plus(left, right):
    return left[0] + right[0], left[1] + right[1]


def minus(left, right):
    return left[0] - right[0], left[1] - right[1]


def negative(value):
    return -value[0], -value[1]


def turned(value):
    return value[0].T, value[1].T


def take(ref, *index):
    return ref[(0,) + index], ref[(1,) + index]


def put(ref, value, *index):
    ref[(0,) + index] = value[0]
    ref[(1,) + index] = value[1]


def invert_small(blocks):
    size = blocks[0][0].shape[0]
    panel = 4 if size % 4 == 0 else 1
    lane = lax.broadcasted_iota(jnp.int32, (1, size), 1)
    row = lax.broadcasted_iota(jnp.int32, (size, 1), 0)
    for start in range(0, size, panel):
        spread = [
            [
                tuple(
                    jnp.broadcast_to(part[:, k : k + 1], (size, size)) for part in parts
                )
                for k in range(start, start + panel)
            ]
            for parts in blocks
        ]
        for at in range(panel):
            k = start + at
            at_lane = lane == k
            at_row = row == k
            after = []
            for (real, imag), columns in zip(blocks, spread):
                col_real, col_imag = columns[at]
                pivot_real = col_real[k : k + 1]
                pivot_imag = col_imag[k : k + 1]
                scale = 1.0 / (pivot_real * pivot_real + pivot_imag * pivot_imag)
                inv_real = pivot_real * scale
                inv_imag = -pivot_imag * scale
                for later in range(at + 1, panel):
                    j = start + later
                    entry_real = col_real[j : j + 1]
                    entry_imag = col_imag[j : j + 1]
                    new_real = inv_real * entry_real - inv_imag * entry_imag
                    new_imag = inv_real * entry_imag + inv_imag * entry_real
                    old_real, old_imag = columns[later]
                    columns[later] = (
                        jnp.where(
                            at_row,
                            new_real,
                            old_real - (col_real * new_real - col_imag * new_imag),
                        ),
                        jnp.where(
                            at_row,
                            new_imag,
                            old_imag - (col_real * new_imag + col_imag * new_real),
                        ),
                    )
                row_real = jnp.where(at_lane, 1.0, real[k : k + 1])
                row_imag = jnp.where(at_lane, 0.0, imag[k : k + 1])
                new_real = inv_real * row_real - inv_imag * row_imag
                new_imag = inv_real * row_imag + inv_imag * row_real
                real = jnp.where(at_lane, 0.0, real) - (col_real * new_real - col_imag * new_imag)
                imag = jnp.where(at_lane, 0.0, imag) - (col_real * new_imag + col_imag * new_real)
                real = jnp.where(at_row, new_real, real)
                imag = jnp.where(at_row, new_imag, imag)
                after.append((real, imag))
            blocks = after
    return blocks


def invert_steps(state, batch, size):
    width = state.shape[-1]
    block = next(s for s in (32, 16, 8, 1) if size % s == 0)

    def step(index, carry):
        low = pl.multiple_of(index * block, block)
        lane = lax.broadcasted_iota(jnp.int32, (block, width), 1)
        row = lax.broadcasted_iota(jnp.int32, (block, width), 0)
        inside = (lane >= low) & (lane < low + block)
        unit = jnp.where(lane == row + low, 1.0, 0.0)
        sign = jnp.where(lane < low, -1.0, 1.0)
        back = lax.rem(width - low, width)
        rows = []
        small = []
        for b in range(batch):
            real = state[b, 0, pl.ds(low, block), :]
            imag = state[b, 1, pl.ds(low, block), :]
            rows.append((real, imag))
            small.append(
                (
                    pltpu.roll(real, back, 1)[:, :block],
                    pltpu.roll(imag, back, 1)[:, :block],
                )
            )
        small = invert_small(small)
        all_lane = lax.broadcasted_iota(jnp.int32, (size, width), 1)
        all_inside = (all_lane >= low) & (all_lane < low + block)
        for b in range(batch):
            real, imag = rows[b]
            new_real, new_imag = complex_dot_rows(
                *small[b], jnp.where(inside, unit, real), jnp.where(inside, 0.0, imag)
            )
            change_real, change_imag = complex_dot_rows(
                (sign * real)[:, :size], (sign * imag)[:, :size], new_real, new_imag
            )
            state[b, 0] = jnp.where(all_inside, 0.0, state[b, 0]) - change_real
            state[b, 1] = jnp.where(all_inside, 0.0, state[b, 1]) - change_imag
            state[b, 0, pl.ds(low, block), :] = new_real
            state[b, 1, pl.ds(low, block), :] = new_imag
        return carry

    lax.fori_loop(0, size // block, step, 0)


def invert_all(state, blocks):
    size = blocks[0][0].shape[0]
    for b, parts in enumerate(blocks):
        for part in range(2):
            state[b, part, :, :size] = 0.5 * (parts[part] + parts[part].T)
            if state.shape[-1] > size:
                state[b, part, :, size:] = jnp.zeros(
                    (size, state.shape[-1] - size), jnp.float32
                )
    invert_steps(state, len(blocks), size)
    return [(state[b, 0, :, :size], state[b, 1, :, :size]) for b in range(len(blocks))]


def run(kernel, out_shapes, inputs, size=0, batch=0, micros=2):
    scratch = []
    if batch:
        scratch = [pltpu.VMEM((batch, 2, size, -(-size // 128) * 128), jnp.float32)]
    return pl.pallas_call(
        kernel,
        out_shape=[jax.ShapeDtypeStruct(shape, jnp.float32) for shape in out_shapes],
        in_specs=[pl.BlockSpec(memory_space=pltpu.VMEM)] * len(inputs),
        out_specs=[pl.BlockSpec(memory_space=pltpu.VMEM)] * len(out_shapes),
        scratch_shapes=scratch,
        compiler_params=pltpu.CompilerParams(vmem_limit_bytes=48 * 1024 * 1024),
        cost_estimate=pl.CostEstimate(
            flops=micros * 1000000000, bytes_accessed=1000000, transcendentals=0
        ),
    )(*inputs)


def local_kernel(
    onsite_ref, hop_ref, real_ref, imag_ref,
    g0_ref, g1_ref, g2_ref, below_ref, above_ref, sb_ref, out_pivot_ref, pivot_ref, state,
):
    count = real_ref.shape[1]
    size = onsite_ref.shape[0]
    eye = lax.broadcasted_iota(jnp.int32, (size, size), 0) == lax.broadcasted_iota(
        jnp.int32, (size, size), 1
    )
    hop = hop_ref[...]
    hop_t = hop.T

    def block(slab, e):
        return (
            jnp.where(eye, real_ref[slab, e : e + 1, :], 0.0) - onsite_ref[...],
            jnp.where(eye, imag_ref[slab, e : e + 1, :], 0.0),
        )

    pairs = invert_all(
        state, [block(0, e) for e in range(count)] + [block(2, e) for e in range(count)]
    )
    middle = []
    for e in range(count):
        g0, g2 = pairs[e], pairs[count + e]
        put(g0_ref, g0, e)
        put(g2_ref, g2, e)
        g0h, g0t = dot_real(g0, hop), dot_real(g0, hop_t)
        g2h, g2t = dot_real(g2, hop), dot_real(g2, hop_t)
        put(below_ref, negative(real_dot(hop_t, g0t)), e)
        put(above_ref, negative(real_dot(hop, g2h)), e)
        put(out_pivot_ref, negative(real_dot(hop, g0t)), e)
        put(pivot_ref, minus(block(3, e), real_dot(hop_t, g2h)), e)
        middle.append(minus(block(1, e), plus(real_dot(hop_t, g0h), real_dot(hop, g2t))))
    for e, g1 in enumerate(invert_all(state, middle)):
        put(g1_ref, g1, e)
        below = take(below_ref, e)
        sb = complex_dot(g1, below)
        put(sb_ref, sb, e)
        put(out_pivot_ref, minus(take(out_pivot_ref, e), complex_dot(turned(below), sb)), e)


def put_pair(ref, right, square, e):
    columns = right[0].shape[-1]
    for part in range(2):
        ref[part, e, :, :columns] = right[part]
        ref[part, e, :, columns:] = square[part]


def take_right(ref, columns, e):
    return ref[0, e, :, :columns], ref[1, e, :, :columns]


def take_square(ref, columns, e):
    return ref[0, e, :, columns:], ref[1, e, :, columns:]


def local_rest_kernel(
    hop_ref, joined_ref, g0_ref, g1_ref, g2_ref, below_ref, above_ref, sb_ref, partial_ref,
    right_ref, z0_ref, z1_ref, z2_ref, sa_ref, pivot_ref, lower_ref, own_ref, out_ref,
):
    hop = hop_ref[...]
    hop_t = hop.T
    for e in range(g0_ref.shape[1]):
        b0, b1, b2, b3 = (
            (right_ref[slab, 0, e], right_ref[slab, 1, e]) for slab in range(4)
        )
        g1 = take(g1_ref, e)
        above = take(above_ref, e)
        above_t = turned(above)
        sa = complex_dot(g1, above)
        put(sa_ref, sa, e)
        put(pivot_ref, minus(take(partial_ref, e), complex_dot(above_t, sa)), e)
        lower = tuple(
            jnp.where(joined_ref[...] > 0, -part, 0.0)
            for part in complex_dot(above_t, take(sb_ref, e))
        )
        put(lower_ref, lower, e)
        z0 = complex_dot(take(g0_ref, e), b0)
        z2 = complex_dot(take(g2_ref, e), b2)
        b1 = plus(b1, plus(real_dot(hop_t, z0), real_dot(hop, z2)))
        z1 = complex_dot(g1, b1)
        put(z0_ref, z0, e)
        put(z1_ref, z1, e)
        put(z2_ref, z2, e)
        put_pair(
            out_ref,
            minus(real_dot(hop, z0), complex_dot(turned(take(below_ref, e)), z1)),
            turned(lower),
            e,
        )
        put(own_ref, minus(plus(b3, real_dot(hop_t, z2)), complex_dot(above_t, z1)), e)


def first_kernel(own_ref, more_ref, pivot_ref, g_ref, state):
    count = own_ref.shape[1]
    for e in range(count):
        put(pivot_ref, plus(take(own_ref, e), take(more_ref, e)), e)
    inverse = invert_all(state, [take(pivot_ref, e) for e in range(count)])
    for e in range(count):
        put(g_ref, inverse[e], e)


def level_kernel(old_ref, lower_ref, upper_ref, below_ref, above_ref, pivot_ref, g_ref, state):
    count = old_ref.shape[1]
    for e in range(count):
        change = plus(
            complex_dot(take(lower_ref, e), take(below_ref, e)),
            complex_dot(take(upper_ref, e), take(above_ref, e)),
        )
        put(pivot_ref, minus(take(old_ref, e), change), e)
    inverse = invert_all(state, [take(pivot_ref, e) for e in range(count)])
    for e in range(count):
        put(g_ref, inverse[e], e)


def last_kernel(old_ref, link_ref, other_ref, pivot_ref, g_ref, state):
    count = old_ref.shape[1]
    for e in range(count):
        change = complex_dot(take(link_ref, e), take(other_ref, e))
        put(pivot_ref, minus(take(old_ref, e), change), e)
    inverse = invert_all(state, [take(pivot_ref, e) for e in range(count)])
    for e in range(count):
        put(g_ref, inverse[e], e)


def scale_kernel(g_ref, lower_ref, rest_ref, xl_ref, xu_ref):
    columns = rest_ref.shape[-1] - lower_ref.shape[-1]
    for e in range(g_ref.shape[1]):
        g = take(g_ref, e)
        put(xl_ref, complex_dot(g, take(lower_ref, e)), e)
        put(xu_ref, complex_dot(g, take_square(rest_ref, columns, e)), e)


def rest_kernel(g_ref, xl_ref, xu_ref, own_ref, rest_ref, right_ref, up_ref, down_ref):
    columns = own_ref.shape[-1]
    for e in range(g_ref.shape[1]):
        right = plus(take(own_ref, e), take_right(rest_ref, columns, e))
        put(right_ref, right, e)
        x = complex_dot(take(g_ref, e), right)
        put_pair(up_ref, x, take(xl_ref, e), e)
        put_pair(down_ref, x, take(xu_ref, e), e)


def rescale_kernel(
    g_ref, lower_ref, upper_ref, below_ref, above_ref,
    new_lower_ref, new_upper_ref, xl_ref, xu_ref,
):
    columns = below_ref.shape[-1] - lower_ref.shape[-1]
    for e in range(g_ref.shape[1]):
        g = take(g_ref, e)
        lower = negative(complex_dot(take(lower_ref, e), take_square(below_ref, columns, e)))
        upper = negative(complex_dot(take(upper_ref, e), take_square(above_ref, columns, e)))
        put(new_lower_ref, lower, e)
        put(new_upper_ref, upper, e)
        put(xl_ref, complex_dot(g, lower), e)
        put(xu_ref, complex_dot(g, upper), e)


def rescale_last_kernel(g_ref, lower_ref, upper_ref, below_ref, above_ref, link_ref, x_ref):
    columns = below_ref.shape[-1] - lower_ref.shape[-1]
    for e in range(g_ref.shape[1]):
        link = negative(
            plus(
                complex_dot(take(lower_ref, e), take_square(below_ref, columns, e)),
                complex_dot(take(upper_ref, e), take_square(above_ref, columns, e)),
            )
        )
        put(link_ref, link, e)
        put(x_ref, complex_dot(take(g_ref, e), link), e)


def right_change(lower_ref, upper_ref, below_ref, above_ref, e):
    columns = below_ref.shape[-1] - lower_ref.shape[-1]
    return plus(
        complex_dot(take(lower_ref, e), take_right(below_ref, columns, e)),
        complex_dot(take(upper_ref, e), take_right(above_ref, columns, e)),
    )


def rest_again_kernel(
    g_ref, lower_ref, upper_ref, below_ref, above_ref, old_ref, xl_ref, xu_ref,
    right_ref, up_ref, down_ref,
):
    for e in range(g_ref.shape[1]):
        right = minus(
            take(old_ref, e), right_change(lower_ref, upper_ref, below_ref, above_ref, e)
        )
        put(right_ref, right, e)
        x = complex_dot(take(g_ref, e), right)
        put_pair(up_ref, x, take(xl_ref, e), e)
        put_pair(down_ref, x, take(xu_ref, e), e)


def rest_last_kernel(
    g_ref, lower_ref, upper_ref, below_ref, above_ref, old_ref, right_ref, x_ref
):
    for e in range(g_ref.shape[1]):
        right = minus(
            take(old_ref, e), right_change(lower_ref, upper_ref, below_ref, above_ref, e)
        )
        put(right_ref, right, e)
        put(x_ref, complex_dot(take(g_ref, e), right), e)


def final_kernel(g_ref, link_ref, other_ref, right_ref, x_ref):
    for e in range(g_ref.shape[1]):
        change = complex_dot(take(link_ref, e), take(other_ref, e))
        put(x_ref, complex_dot(take(g_ref, e), minus(take(right_ref, e), change)), e)


def middle_kernel(z1_ref, sb_ref, sa_ref, previous_ref, x3_ref, x1_ref):
    for e in range(z1_ref.shape[1]):
        change = plus(
            complex_dot(take(sb_ref, e), take(previous_ref, e)),
            complex_dot(take(sa_ref, e), take(x3_ref, e)),
        )
        put(x1_ref, minus(take(z1_ref, e), change), e)


def outer_kernel(
    hop_ref, g0_ref, g2_ref, z0_ref, z2_ref, previous_ref, x1_ref, x3_ref, x0_ref, x2_ref
):
    hop = hop_ref[...]
    hop_t = hop.T
    for e in range(z0_ref.shape[1]):
        x1 = take(x1_ref, e)
        for_0 = plus(real_dot(hop_t, take(previous_ref, e)), real_dot(hop, x1))
        for_2 = plus(real_dot(hop_t, x1), real_dot(hop, take(x3_ref, e)))
        put(x0_ref, plus(take(z0_ref, e), complex_dot(take(g0_ref, e), for_0)), e)
        put(x2_ref, plus(take(z2_ref, e), complex_dot(take(g2_ref, e), for_2)), e)


def per_device(
    source,
    onsite_block,
    hopping_block,
    potential_table,
    slab_profile,
    occupation,
    coupling,
    phonon_shift,
):
    slab_count = occupation.shape[0]
    energy_count = occupation.shape[1]
    orbitals = onsite_block.shape[0]
    half = energy_count // 2
    if slab_count != 2 or energy_count % 2 or lax.axis_size("slab") % 2:
        raise ValueError("unsupported shape")
    hop = hopping_block
    place = lax.axis_index("slab")
    upper_half = (place % 2) == 1
    widened = padded(occupation, (("energy", 1),), energy_count)
    own_points = jnp.arange(energy_count, dtype=jnp.int32)[:, None]
    all_points = jnp.arange(3 * energy_count, dtype=jnp.int32)[None, :]
    weights = jnp.zeros((energy_count, 3 * energy_count), jnp.float32)
    for mode in range(phonon_shift.shape[0]):
        above = (all_points == own_points + energy_count + phonon_shift[mode]).astype(jnp.float32)
        below = (all_points == own_points + energy_count - phonon_shift[mode]).astype(jnp.float32)
        weights = weights + coupling[mode] * (above + below)
    damping = jnp.sum(weights[None, :, :, None] * widened[:, None], axis=2)
    chosen = (
        slab_profile[:, None] == jnp.arange(potential_table.shape[0], dtype=jnp.int32)[None, :]
    )
    potential = jnp.sum(jnp.where(chosen[..., None], potential_table[None], 0.0), axis=1)

    def exchanged(array, axis):
        low = lax.slice_in_dim(array, 0, half, axis=axis)
        high = lax.slice_in_dim(array, half, energy_count, axis=axis)
        kept = jnp.where(upper_half, high, low)
        other = swapped(jnp.where(upper_half, low, high), "slab")
        return kept, other

    def ordered(kept, other):
        return jnp.where(
            upper_half,
            jnp.concatenate([other, kept], axis=0),
            jnp.concatenate([kept, other], axis=0),
        )

    shared = jnp.concatenate(
        [damping, jnp.broadcast_to(potential[:, None], damping.shape)], axis=-1
    )
    shared = ordered(*exchanged(shared, 1))
    damping = shared[..., :orbitals]
    potential = shared[..., orbitals:]
    right = ordered(*exchanged(source, 2))

    first_point = lax.axis_index("energy") * energy_count + jnp.where(upper_half, half, 0)
    energies = energy_low + energy_step * (
        first_point + jnp.arange(half, dtype=jnp.int32)
    ).astype(jnp.float32)
    real_diag = energies[None, :, None] - potential
    imag_diag = broadening + damping
    square = (2, half, orbitals, orbitals)
    tall = (2, half, orbitals, source.shape[-1])
    columns = source.shape[-1]
    wide = (2, half, orbitals, columns + orbitals)
    count = lax.axis_size("slab") // 2
    if count < 4 or count & (count - 1):
        raise ValueError("unsupported mesh")
    g0, g1, g2, below, above, sb, out_pivot, partial = run(
        local_kernel,
        [square] * 8,
        [onsite_block, hop, real_diag, imag_diag],
        orbitals,
        2 * half,
        30,
    )
    joined = jnp.full((1, orbitals), place // 2, jnp.int32)
    more = shifted(out_pivot, "slab", -2)
    z0, z1, z2, sa, pivot, lower, right_now, out_rest = run(
        local_rest_kernel,
        [tall, tall, tall, square, square, square, tall, wide],
        [hop, joined, g0, g1, g2, below, above, sb, partial, right],
    )
    more, out_rest = lax.optimization_barrier((more, out_rest))
    rest = shifted(out_rest, "slab", -2)
    pivot, inverse = run(first_kernel, [square] * 2, [pivot, more], orbitals, half, 14)
    x_lower, x_upper = run(scale_kernel, [square] * 2, [inverse, lower, rest])
    upper = rest[..., columns:]
    distance = 2
    below_upper = shifted(x_upper, "slab", distance)
    above_lower = shifted(x_lower, "slab", -distance)
    right_now, up, down = run(
        rest_kernel, [tall, wide, wide], [inverse, x_lower, x_upper, right_now, rest]
    )
    while True:
        below_upper, above_lower, up, down = lax.optimization_barrier(
            (below_upper, above_lower, up, down)
        )
        below_rest = shifted(up, "slab", distance)
        above_rest = shifted(down, "slab", -distance)
        pivot, inverse = run(
            level_kernel,
            [square] * 2,
            [pivot, lower, upper, below_upper, above_lower],
            orbitals,
            half,
            14,
        )
        distance *= 2
        if distance == count:
            break
        new_lower, new_upper, x_lower, x_upper = run(
            rescale_kernel, [square] * 4, [inverse, lower, upper, below_rest, above_rest]
        )
        below_upper = shifted(x_upper, "slab", distance)
        above_lower = shifted(x_lower, "slab", -distance)
        right_now, up, down = run(
            rest_again_kernel,
            [tall, wide, wide],
            [inverse, lower, upper, below_rest, above_rest, right_now, x_lower, x_upper],
        )
        lower, upper = new_lower, new_upper
    partners = [(i, (i + count) % (2 * count)) for i in range(2 * count)]
    link, x = run(
        rescale_last_kernel, [square] * 2, [inverse, lower, upper, below_rest, above_rest]
    )
    other = lax.ppermute(x, "slab", partners)
    right_now, x_right = run(
        rest_last_kernel,
        [tall] * 2,
        [inverse, lower, upper, below_rest, above_rest, right_now],
    )
    other, x_right = lax.optimization_barrier((other, x_right))
    other_right = lax.ppermute(x_right, "slab", partners)
    pivot, inverse = run(last_kernel, [square] * 2, [pivot, link, other], orbitals, half, 14)
    (x3,) = run(final_kernel, [tall], [inverse, link, other_right, right_now])
    previous = shifted(x3, "slab", 2)
    (x1,) = run(middle_kernel, [tall], [z1, sb, sa, previous, x3])
    first = swapped(jnp.where(upper_half, x1, x3), "slab")
    x0, x2 = run(outer_kernel, [tall] * 2, [hop, g0, g2, z0, z2, previous, x1, x3])
    second = swapped(jnp.where(upper_half, x0, x2), "slab")
    kept = jnp.where(upper_half, jnp.stack([x2, x3]), jnp.stack([x0, x1]))
    other = jnp.stack([second, first])
    amplitude = jnp.where(
        upper_half,
        jnp.concatenate([other, kept], axis=2),
        jnp.concatenate([kept, other], axis=2),
    )
    density = jnp.sum(amplitude[:, 0] ** 2 + amplitude[:, 1] ** 2, axis=-1)
    return (amplitude, density)


def solution(mesh):
    placed = (
        P("slab", None, "energy", None, None),
        P(),
        P(),
        P(),
        P("slab"),
        P("slab", "energy", None),
        P(),
        P(),
    )
    return jax.shard_map(
        per_device,
        mesh=mesh,
        in_specs=placed,
        out_specs=(P("slab", None, "energy", None, None), P("slab", "energy", None)),
        check_vma=False,
    )
```
